512 devices in a mesh: blk: 32 (over x, z_lo), feat: 16 (over z_hi, y, core).
Axes of the slice: x: 4, y: 4, z: 16 (z_hi: 2, z_lo: 8; z = z_hi * 8 + z_lo), core: 2. Of those that a mesh axis runs over, the one named last changes fastest.
Arguments:
- values: bfloat16 [16384, 8192], P('blk', 'feat'), may hold values from -6 to 6
- scales: float32 [16384, 64], P('blk', 'feat'), may hold values from 0.25 to 4
- pairing: int32 [2], replicated, may hold values from 1 to 31
Outputs:
- similarity: float32 [2, 16384, 512], P(None, 'blk', 'feat')
The draws below stay inside these ranges and needn't reach their ends.
All inputs are finite; a program needn't handle non-finite values.
Results may differ from the reference program's by a relative error of at most 0.017.
Values may be sent and summed in bfloat16 or wider, within the bound.
A program may use at most 64 MiB of HBM per device.

```python
import math
import jax
import jax.numpy as jnp
from jax import lax

BLOCK_ROWS = 512
FEATURES = 8192
GROUP = 128
ROUNDS = 2
EXAMPLES = 16384
GROUPS = 64
N_BLK = 32


def block_scale(key, shape, cuts, smallest, largest):
    def one(axis_at, shards_of):
        heights = jax.random.uniform(jax.random.fold_in(jax.random.fold_in(key, 6), axis_at), (shards_of,), jnp.float32, smallest / len(cuts), largest / len(cuts))
        return jnp.repeat(jnp.exp(heights), shape[axis_at] // shards_of).reshape((-1,) + (1,) * (len(shape) - axis_at - 1))

    gain = one(*cuts[0])
    for cut in cuts[1:]:
        gain = gain * one(*cut)
    return gain


def normal_values(rng, dims, spread, bound, cuts=(), held_as=jnp.bfloat16):
    gain = block_scale(rng, dims, cuts, -0.22, 0.18) if cuts else 1.0
    result = jax.random.normal(rng, dims, jnp.float32) * spread * gain
    return jnp.minimum(jnp.maximum(result, -bound), bound).astype(held_as)


def setup_inputs(seed: int = 0) -> dict:
    key_list = jax.random.split(jax.random.key(seed), 4)
    return {
        "values": normal_values(key_list[0], (EXAMPLES, FEATURES), 1.0, 6.0, ((0, 32), (1, 16))),
        "scales": jnp.clip(jnp.exp(math.log(4.0) - 2.7725887 * jax.random.uniform(key_list[1], (EXAMPLES, GROUPS), jnp.float32) ** block_scale(key_list[1], (EXAMPLES, GROUPS), ((0, 32), (1, 16)), -0.2, 0.2)), 0.25, 4.0),
        "pairing": jax.random.randint(key_list[2], (ROUNDS,), 1, N_BLK).astype(jnp.int32),
    }


eps = 1e-06

def reference(values, scales, pairing):
    wide = values.astype(jnp.float32).reshape(EXAMPLES, GROUPS, GROUP) * scales[:, :, None]
    features = wide.reshape(EXAMPLES, FEATURES).astype(jnp.bfloat16)
    sumsq = lax.optimization_barrier(jnp.sum(jnp.square(features.astype(jnp.float32)), axis=1))
    inverse = lax.rsqrt(sumsq + eps)
    blocks = features.reshape(N_BLK, BLOCK_ROWS, FEATURES)
    inv_blocks = inverse.reshape(N_BLK, BLOCK_ROWS)
    factor = jnp.float32(FEATURES) ** 0.5

    def one_round(offset):

        def one_block(index):
            other = jnp.remainder(index + offset, N_BLK).astype(jnp.int32)
            gram = lax.dot_general(blocks[index], blocks[other], (((1,), (1,)), ((), ())), preferred_element_type=jnp.float32)
            return gram * inv_blocks[index][:, None] * inv_blocks[other][None, :] * factor
        tiles = lax.map(one_block, jnp.arange(N_BLK, dtype=jnp.int32))
        return tiles.reshape(EXAMPLES, BLOCK_ROWS)
    return jnp.stack([one_round(pairing[step]) for step in range(ROUNDS)])
```

```python
import functools

import jax
import jax.numpy as jnp
from jax import lax
from jax.experimental import pallas as pl
from jax.experimental.pallas import tpu as pltpu
from jax.sharding import PartitionSpec as P

FEATURES = 8192
ROUNDS = 2
EPS = 1e-06
N_BLK = 32
MESH = pl.DeviceIdType.MESH


def fetch_kernel(offset, pieces, src, dst, send, recv):
    blk = lax.axis_index("blk")
    source = lax.rem(blk + offset, N_BLK)
    target = lax.rem(blk + (N_BLK - offset), N_BLK)
    barrier = pltpu.get_barrier_semaphore()
    pl.semaphore_signal(barrier, inc=1, device_id={"blk": source}, device_id_type=MESH)
    pl.semaphore_wait(barrier, 1)
    rows = src.shape[0] // pieces
    copies = []
    for piece in range(pieces):
        part = pl.ds(piece * rows, rows)
        copy = pltpu.make_async_remote_copy(
            src_ref=src.at[part], dst_ref=dst.at[part], send_sem=send.at[piece], recv_sem=recv.at[piece],
            device_id={"blk": target}, device_id_type=MESH,
        )
        copy.start()
        copies.append(copy)
    for copy in copies:
        copy.wait()


def fetch(offset, features):
    pieces = 1
    return pl.pallas_call(
        functools.partial(fetch_kernel, offset, pieces),
        out_shape=jax.ShapeDtypeStruct(features.shape, features.dtype),
        in_specs=[pl.BlockSpec(memory_space=pl.ANY)],
        out_specs=pl.BlockSpec(memory_space=pl.ANY),
        scratch_shapes=[pltpu.SemaphoreType.DMA((pieces,)), pltpu.SemaphoreType.DMA((pieces,))],
        compiler_params=pltpu.CompilerParams(collective_id=offset, has_side_effects=True),
        name=f"fetch_{offset}",
    )(features)


def dot_t(a, b):
    return lax.dot_general(a, b, (((1,), (1,)), ((), ())), preferred_element_type=jnp.float32)


def square_sums(block):
    wide = block.astype(jnp.float32)
    square = wide * wide
    high = square.astype(jnp.bfloat16)
    low = (square - high.astype(jnp.float32)).astype(jnp.bfloat16)
    ones = jnp.ones((8, block.shape[1]), jnp.bfloat16)
    return dot_t(ones, high) + dot_t(ones, low)


def gram_kernel(own_ref, first_ref, second_ref, out_ref,
                mine, s1, r1, s2, r2, s3, r3, n0, n1, n2, n3,
                send1, recv1, send2, recv2, send3, recv3):
    feat = lax.axis_index("feat")
    core = lax.rem(feat, 2)
    y = lax.rem(feat // 2, 4)
    half = feat // 8
    to_core = feat + 1 - 2 * core
    to_half = feat + 8 - 16 * half
    to_y = [feat + 2 * (lax.rem(y + t, 4) - y) for t in (1, 2, 3)]

    barrier = pltpu.get_barrier_semaphore()
    for peer in [to_core, to_half] + to_y:
        pl.semaphore_signal(barrier, inc=1, device_id={"feat": peer}, device_id_type=MESH)
    partners = (first_ref, second_ref)

    def remote(src, dst, send, recv, peer):
        return pltpu.make_async_remote_copy(
            src_ref=src, dst_ref=dst, send_sem=send, recv_sem=recv,
            device_id={"feat": peer}, device_id_type=MESH)

    own = own_ref[...]
    stage1 = []
    for r in range(ROUNDS):
        rows = partners[r][:, 1 - core].reshape(256, 512)
        s1[r] = dot_t(rows, own).astype(jnp.bfloat16).reshape(8, 32, 512)
        if r == 0:
            pl.semaphore_wait(barrier, 5)
        copy = remote(s1.at[r], r1.at[r], send1.at[r], recv1.at[r], to_core)
        copy.start()
        stage1.append(copy)
    row = lax.broadcasted_iota(jnp.int32, (8, 512), 0)
    sums = [square_sums(own)] + [square_sums(p[...].reshape(512, 512)) for p in partners]
    n0[...] = jnp.where(row == 0, sums[0], jnp.where(row == 1, sums[1], sums[2]))
    copy = remote(n0, n1.at[0], send1.at[2], recv1.at[2], to_core)
    copy.start()
    stage1.append(copy)
    for r in range(ROUNDS):
        rows = partners[r][:, core].reshape(256, 512)
        mine[r] = dot_t(rows, own).reshape(8, 32, 512)

    for copy in stage1:
        copy.wait_recv()
    stage2 = []
    n1[1] = n0[...] + n1[0]
    for t in (1, 2, 3):
        there = lax.rem(y + t, 4)
        for r in range(ROUNDS):
            for h in range(2):
                q = h * 4 + there
                s2[t - 1, r, h] = (mine[r, q] + r1[r, q].astype(jnp.float32)).astype(jnp.bfloat16)
        for src, dst, k in ((s2.at[t - 1], r2.at[t - 1], 0), (n1.at[1], n2.at[t - 1], 1)):
            copy = remote(src, dst, send2.at[t - 1, k], recv2.at[t - 1, k], to_y[t - 1])
            copy.start()
            stage2.append(copy)
    for copy in stage2:
        copy.wait_recv()

    def total(r, h):
        q = h * 4 + y
        value = mine[r, q] + r1[r, q].astype(jnp.float32)
        for t in range(3):
            value = value + r2[t, r, h].astype(jnp.float32)
        return value

    n3[0] = n1[1] + n2[0] + n2[1] + n2[2]
    for r in range(ROUNDS):
        s3[r] = total(r, 1 - half).astype(jnp.bfloat16)
    stage3 = [remote(s3, r3, send3.at[0], recv3.at[0], to_half),
              remote(n3.at[0], n3.at[1], send3.at[1], recv3.at[1], to_half)]
    for copy in stage3:
        copy.start()
    for r in range(ROUNDS):
        mine[r, 0] = total(r, half)
    for copy in stage3:
        copy.wait_recv()
    inverse = lax.rsqrt(n3[0] + n3[1] + EPS)
    lane = lax.broadcasted_iota(jnp.int32, (32, 512), 1)
    at = lax.broadcasted_iota(jnp.int32, (32, 512), 0) + feat * 32
    factor = jnp.float32(FEATURES) ** 0.5
    for r in range(ROUNDS):
        spread = jnp.broadcast_to(inverse[1 + r:2 + r], (32, 512))
        column = jnp.sum(jnp.where(lane == at, spread, 0.0), axis=1, keepdims=True)
        gram = mine[r, 0] + r3[r].astype(jnp.float32)
        out_ref[r] = gram * inverse[0:1] * column * factor
    for copy in stage1 + stage2 + stage3:
        copy.wait_send()


def grams(own, first, second):
    bf16, f32 = jnp.bfloat16, jnp.float32
    vmem = pl.BlockSpec(memory_space=pltpu.VMEM)
    return pl.pallas_call(
        gram_kernel,
        out_shape=jax.ShapeDtypeStruct((ROUNDS, 32, 512), f32),
        in_specs=[vmem] * 3,
        out_specs=vmem,
        scratch_shapes=[
            pltpu.VMEM((ROUNDS, 8, 32, 512), f32),
            pltpu.VMEM((ROUNDS, 8, 32, 512), bf16),
            pltpu.VMEM((ROUNDS, 8, 32, 512), bf16),
            pltpu.VMEM((3, ROUNDS, 2, 32, 512), bf16),
            pltpu.VMEM((3, ROUNDS, 2, 32, 512), bf16),
            pltpu.VMEM((ROUNDS, 32, 512), bf16),
            pltpu.VMEM((ROUNDS, 32, 512), bf16),
            pltpu.VMEM((8, 512), f32),
            pltpu.VMEM((2, 8, 512), f32),
            pltpu.VMEM((3, 8, 512), f32),
            pltpu.VMEM((2, 8, 512), f32),
            pltpu.SemaphoreType.DMA((3,)),
            pltpu.SemaphoreType.DMA((3,)),
            pltpu.SemaphoreType.DMA((3, 2)),
            pltpu.SemaphoreType.DMA((3, 2)),
            pltpu.SemaphoreType.DMA((2,)),
            pltpu.SemaphoreType.DMA((2,)),
        ],
        compiler_params=pltpu.CompilerParams(
            collective_id=0, has_side_effects=True, vmem_limit_bytes=32 * 1024 * 1024),
        name="grams",
    )(own, first.reshape(8, 2, 32, 512), second.reshape(8, 2, 32, 512))


def local(values, scales, pairing):
    rows, width = values.shape
    groups = scales.shape[1]
    wide = values.astype(jnp.float32).reshape(rows, groups, width // groups) * scales[:, :, None]
    features = wide.reshape(rows, width).astype(jnp.bfloat16)
    fetches = [functools.partial(fetch, offset) for offset in range(1, N_BLK)]
    others = [lax.switch(pairing[r] - 1, fetches, features) for r in range(ROUNDS)]
    tiles = grams(features, *others)
    return jnp.swapaxes(tiles, 1, 2)


def solution(mesh):
    placed = (P("blk", "feat"), P("blk", "feat"), P())
    return jax.shard_map(
        local, mesh=mesh, in_specs=placed, out_specs=P(None, "blk", "feat"), check_vma=False
    )
```

```python
import functools

import jax
import jax.numpy as jnp
from jax import lax
from jax.experimental import pallas as pl
from jax.experimental.pallas import tpu as pltpu
from jax.sharding import PartitionSpec as P

FEATURES = 8192
GROUP = 128
ROUNDS = 2
EPS = 1e-06
N_BLK = 32
NY = 4
MESH = pl.DeviceIdType.MESH
VMEM = pl.BlockSpec(memory_space=pltpu.VMEM)
BF16, F32 = jnp.bfloat16, jnp.float32


def remote(src, dst, send, recv, peer):
    return pltpu.make_async_remote_copy(
        src_ref=src, dst_ref=dst, send_sem=send, recv_sem=recv, device_id=peer, device_id_type=MESH)


def fetch_kernel(offset, low_ref, high_ref, part_ref, other_ref, wide_ref, send, recv, send_y, recv_y):
    blk, feat = lax.axis_index("blk"), lax.axis_index("feat")
    source = lax.rem(blk + offset, N_BLK)
    target = lax.rem(blk + (N_BLK - offset), N_BLK)
    y = lax.rem(feat // 2, NY)
    ys = [lax.rem(y + t, NY) for t in range(NY)]
    feats = [feat + 2 * (there - y) for there in ys]
    barrier = pltpu.get_barrier_semaphore()
    for t in range(NY):
        pl.semaphore_signal(barrier, inc=1, device_id={"blk": source, "feat": feats[t]}, device_id_type=MESH)
    for t in range(1, NY):
        pl.semaphore_signal(barrier, inc=1, device_id={"blk": blk, "feat": feats[t]}, device_id_type=MESH)
    wide_ref[y] = part_ref[...]
    pl.semaphore_wait(barrier, 2 * NY - 1)
    copies = []
    for t in range(NY):
        for h, src in enumerate((low_ref, high_ref)):
            copies.append(remote(src.at[ys[t]], other_ref.at[y, h], send.at[t, h], recv.at[t, h],
                                 {"blk": target, "feat": feats[t]}))
    for t in (1, 3, 2):
        copies.append(remote(part_ref, wide_ref.at[y], send_y.at[t - 1], recv_y.at[t - 1],
                             {"blk": blk, "feat": feats[t]}))
    for copy in copies:
        copy.start()
    for copy in copies:
        copy.wait()


def fetch(offset, low, high, part):
    dma = pltpu.SemaphoreType.DMA
    return pl.pallas_call(
        functools.partial(fetch_kernel, offset),
        out_shape=(jax.ShapeDtypeStruct((NY, 2, 2, 32, 512), BF16), jax.ShapeDtypeStruct((NY, 256, 512), BF16)),
        in_specs=[VMEM] * 3,
        out_specs=(VMEM, VMEM),
        scratch_shapes=[dma((NY, 2)), dma((NY, 2)), dma((NY - 1,)), dma((NY - 1,))],
        compiler_params=pltpu.CompilerParams(collective_id=offset, has_side_effects=True),
        name=f"fetch_{offset}",
    )(low.reshape(NY, 2, 32, 512), high.reshape(NY, 2, 32, 512), part)


def dot_t(a, b):
    return lax.dot_general(a, b, (((1,), (1,)), ((), ())), preferred_element_type=F32)


def square_sums(blocks):
    square = sum(jnp.square(block.astype(F32)) for block in blocks)
    high = square.astype(BF16)
    low = (square - high.astype(F32)).astype(BF16)
    ones = jnp.ones((8, square.shape[1]), BF16)
    return dot_t(ones, high) + dot_t(ones, low)


def gram_kernel(first_ref, second_ref, low_ref, high_ref, out_ref,
                mine, s1, r1, s2, r2, n1, n2, send1, recv1, send2, recv2):
    blk, feat = lax.axis_index("blk"), lax.axis_index("feat")
    core = lax.rem(feat, 2)
    half = feat // 8
    to_core = {"blk": blk, "feat": feat + 1 - 2 * core}
    to_half = {"blk": blk, "feat": feat + 8 - 16 * half}
    barrier = pltpu.get_barrier_semaphore()
    for peer in (to_core, to_half):
        pl.semaphore_signal(barrier, inc=1, device_id=peer, device_id_type=MESH)

    owns = (low_ref, high_ref)
    rows = [jnp.concatenate([ref[y].reshape(128, 512) for ref in (first_ref, second_ref)]) for y in range(NY)]
    stage1, stage2 = [], []
    for a in range(2):
        product = dot_t(rows[0], owns[a][0])
        for y in range(1, NY):
            product = product + dot_t(rows[y], owns[a][y])
        mine[a] = product.reshape(ROUNDS, 2, 2, 32, 256)
        s1[a] = mine[a, :, :, 1 - core].astype(BF16)
        if a == 0:
            pl.semaphore_wait(barrier, 2)
        copy = remote(s1.at[a], r1.at[a], send1.at[a], recv1.at[a], to_core)
        copy.start()
        stage1.append(copy)

    row = lax.broadcasted_iota(jnp.int32, (8, 128), 0)
    sums = [square_sums([owns[a][y] for y in range(NY)]) for a in range(2)]
    lines = [sums[0][:, :128], sums[0][:, 128:], sums[1][:, :128], sums[1][:, 128:]]
    lines += [square_sums([ref[y].reshape(128, 512) for y in range(NY)]) for ref in (first_ref, second_ref)]
    value = lines[0]
    for k in range(1, 6):
        value = jnp.where(row == k, lines[k], value)
    n1[0] = value
    copy = remote(n1.at[0], n1.at[1], send1.at[2], recv1.at[2], to_core)
    copy.start()
    stage1.append(copy)

    for a in range(2):
        stage1[a].wait_recv()
        s2[a] = (mine[a, :, 1 - half, core] + r1[a, :, 1 - half].astype(F32)).astype(BF16)
        copy = remote(s2.at[a], r2.at[a], send2.at[a], recv2.at[a], to_half)
        copy.start()
        stage2.append(copy)
    stage1[2].wait_recv()
    n2[0] = n1[0] + n1[1]
    copy = remote(n2.at[0], n2.at[1], send2.at[2], recv2.at[2], to_half)
    copy.start()
    stage2.append(copy)
    kept = [mine[a, :, half, core] + r1[a, :, half].astype(F32) for a in range(2)]

    stage2[2].wait_recv()
    inverse = lax.rsqrt(n2[0] + n2[1] + EPS)
    lane = lax.broadcasted_iota(jnp.int32, (32, 128), 1)
    at = lax.broadcasted_iota(jnp.int32, (32, 128), 0) + (half * 2 + core) * 32
    factor = F32(FEATURES) ** 0.5
    columns = []
    for r in range(ROUNDS):
        spread = jnp.broadcast_to(inverse[4 + r:5 + r], (32, 128))
        columns.append(jnp.sum(jnp.where(lane == at, spread, 0.0), axis=1, keepdims=True))
    for a in range(2):
        stage2[a].wait_recv()
        gram = kept[a] + r2[a].astype(F32)
        for k in range(2):
            across = inverse[2 * a + k:2 * a + k + 1]
            for r in range(ROUNDS):
                part = gram[r, :, 128 * k:128 * k + 128]
                out_ref[r, :, 256 * a + 128 * k:256 * a + 128 * k + 128] = part * across * columns[r] * factor
    for copy in stage1 + stage2:
        copy.wait_send()


def grams(first, second, low, high):
    dma = pltpu.SemaphoreType.DMA
    return pl.pallas_call(
        gram_kernel,
        out_shape=jax.ShapeDtypeStruct((ROUNDS, 32, 512), F32),
        in_specs=[VMEM] * 4,
        out_specs=VMEM,
        scratch_shapes=[
            pltpu.VMEM((2, ROUNDS, 2, 2, 32, 256), F32),
            pltpu.VMEM((2, ROUNDS, 2, 32, 256), BF16),
            pltpu.VMEM((2, ROUNDS, 2, 32, 256), BF16),
            pltpu.VMEM((2, ROUNDS, 32, 256), BF16),
            pltpu.VMEM((2, ROUNDS, 32, 256), BF16),
            pltpu.VMEM((2, 8, 128), F32),
            pltpu.VMEM((2, 8, 128), F32),
            dma((3,)), dma((3,)), dma((3,)), dma((3,)),
        ],
        compiler_params=pltpu.CompilerParams(
            collective_id=0, has_side_effects=True, vmem_limit_bytes=32 * 1024 * 1024),
        name="grams",
    )(first, second, low, high)


def local(values, scales, pairing):
    rows, width = values.shape
    groups = scales.shape[1]
    wide = values.astype(F32).reshape(rows, groups, width // groups) * scales[:, :, None]
    features = wide.reshape(rows, width).astype(BF16)
    halves = features[:256], features[256:]
    fetches = [functools.partial(fetch, offset) for offset in range(1, N_BLK)]
    (first, low), (second, high) = [
        lax.switch(pairing[r] - 1, fetches, *halves, halves[r]) for r in range(ROUNDS)]
    return jnp.swapaxes(grams(first, second, low, high), 1, 2)


def solution(mesh):
    placed = (P("blk", "feat"), P("blk", "feat"), P())
    return jax.shard_map(
        local, mesh=mesh, in_specs=placed, out_specs=P(None, "blk", "feat"), check_vma=False
    )
```

```python
import functools

import jax
import jax.numpy as jnp
from jax import lax
from jax.experimental import pallas as pl
from jax.experimental.pallas import tpu as pltpu
from jax.sharding import PartitionSpec as P

FEATURES = 8192
GROUP = 128
ROUNDS = 2
EPS = 1e-06
NX, NZ = 4, 8
NY = 4
MESH = pl.DeviceIdType.MESH
VMEM = pl.BlockSpec(memory_space=pltpu.VMEM)
SMEM = pl.BlockSpec(memory_space=pltpu.SMEM)
BF16, F32 = jnp.bfloat16, jnp.float32


def dot_t(a, b):
    return lax.dot_general(a, b, (((1,), (1,)), ((), ())), preferred_element_type=F32)


def kernel(shifts, pairing_ref, values_ref, scales_ref, out_ref,
           held, piece, near, stage, mine, squares, s1, r1, s2, r2, n1, n2,
           send_p, recv_p, send_x, recv_x, send_w, recv_w, send_z, recv_z, send1, recv1, send2, recv2):
    blk, feat = lax.axis_index("blk"), lax.axis_index("feat")
    x, z = blk // NZ, lax.rem(blk, NZ)
    half, y, core = feat // 8, lax.rem(feat // 2, NY), lax.rem(feat, 2)
    to_core = (blk, feat + 1 - 2 * core)
    to_half = (blk, feat + 8 - 16 * half)
    own = held.at[0, pl.ds(0, 2 * NY)]
    moved = [r for r in range(ROUNDS) if shifts[r]]

    def at_y(t):
        return lax.rem(y + NY - t, NY)

    def to_y(t):
        return (blk, feat + 2 * (at_y(t) - y))

    def to_x(s):
        return (lax.rem(x + NX - s, NX) * NZ + z, feat)

    def to_z(d):
        return (x * NZ + lax.rem(z + NZ - d, NZ), feat)

    barrier = pltpu.get_barrier_semaphore()
    sources = [to_z(NZ - d) for d in sorted(set(shifts)) if d]
    peers = [to_y(t) for t in range(1, NY)] + [to_x(s) for s in range(1, NX)] + sources + [to_core, to_half]
    for peer in peers:
        pl.semaphore_signal(barrier, inc=1, device_id=peer, device_id_type=MESH)

    def remote(src, dst, send, recv, peer):
        return pltpu.make_async_remote_copy(
            src_ref=src, dst_ref=dst, send_sem=send, recv_sem=recv, device_id=peer, device_id_type=MESH)

    def piece_copy(t, h):
        return remote(held.at[0, h * NY + at_y(t)], piece.at[t, h],
                      send_p.at[t - 1, h], recv_p.at[t - 1, h], to_y(t))

    def wide_copy(t):
        return remote(own, held.at[t, pl.ds(0, 2 * NY)], send_w.at[t - 1], recv_w.at[t - 1], to_y(t))

    def x_copy(t, s):
        return remote(piece.at[t], near.at[t, s - 1], send_x.at[t, s - 1], recv_x.at[t, s - 1], to_x(s))

    def z_copy(t, r):
        return remote(stage.at[t, r], held.at[t, pl.ds(2 * NY + 2 * r, 2)], send_z.at[t, r], recv_z.at[t, r],
                      to_z(shifts[r]))

    @pl.loop(0, 2 * NY)
    def _(q):
        rows = pl.ds(q * 64, 64)
        for g in range(values_ref.shape[1] // GROUP):
            lanes = slice(g * GROUP, (g + 1) * GROUP)
            part = (values_ref[rows, lanes].astype(F32) * scales_ref[rows, g:g + 1]).astype(BF16)
            held[0, q, :, :, lanes] = part.reshape(2, 32, GROUP)

    for h in range(2):
        piece[0, h] = held[0, h * NY + y]
    pl.semaphore_wait(barrier, len(peers))

    @pl.loop(1, NY)
    def _(t):
        for h in range(2):
            piece_copy(t, h).start()

    first = pairing_ref[0]
    second = pairing_ref[1]
    swap = lax.rem(first, NZ) > lax.rem(second, NZ)
    offsets = [jnp.where(swap, second, first), jnp.where(swap, first, second)]
    picks = [lax.rem(offsets[r] // NZ + jnp.where(z < shifts[r], 1, 0), NX) for r in range(ROUNDS)]

    @pl.loop(0, NY + 1)
    def _(later):
        @pl.when(jnp.logical_and(later > 0, later < NY))
        def _():
            for h in range(2):
                piece_copy(later, h).wait_recv()

        @pl.when(later < NY)
        def _():
            @pl.loop(1, NX)
            def _(s):
                x_copy(later, s).start()

        @pl.when(later == 0)
        def _():
            @pl.loop(1, NY)
            def _(t):
                wide_copy(t).start()

        @pl.when(later > 0)
        def _():
            t = later - 1

            @pl.loop(1, NX)
            def _(s):
                x_copy(t, s).wait_recv()

            for r in range(ROUNDS):
                @pl.loop(0, 4)
                def _(q):
                    h, c = q // 2, lax.rem(q, 2)
                    value = piece[t, h, c]
                    for s in range(1, NX):
                        value = lax.select(picks[r] == s, near[t, s - 1, h, c], value)
                    if shifts[r]:
                        stage[t, r, h, c] = value
                    else:
                        held[t, 2 * NY + 2 * r + h, c] = value

                if shifts[r]:
                    z_copy(t, r).start()

    @pl.loop(1, NY)
    def _(t):
        wide_copy(t).wait_recv()

    @pl.loop(0, 2)
    def _(k):
        mine[k] = jnp.zeros(mine.shape[1:], F32)

    ones = jnp.ones((8, 512), BF16)
    row = lax.broadcasted_iota(jnp.int32, (8, 128), 0)
    stage1 = remote(s1, r1, send1.at[0], recv1.at[0], to_core)
    n1[0] = jnp.zeros((8, 128), F32)

    @pl.loop(0, 2)
    def _(late):
        @pl.when(late == 1)
        def _():
            @pl.loop(0, NY)
            def _(t):
                for r in moved:
                    z_copy(t, r).wait_recv()
                rows = held[t, pl.ds(2 * NY, 4)].reshape(256, 512)

                @pl.loop(0, 2)
                def _(k):
                    owns = held[t, pl.ds(k * NY, NY)].reshape(256, 512)
                    mine[k] += dot_t(rows, owns).reshape(ROUNDS, 2, 2, 32, 256)

            @pl.loop(0, 2)
            def _(k):
                s1[k] = mine[k, :, :, 1 - core].astype(BF16)

            stage1.start()

        @pl.loop(4 * late, 4 + 2 * late)
        def _(k):
            squares[...] = jnp.zeros_like(squares)

            @pl.loop(0, NY)
            def _(t):
                squares[...] += jnp.square(held[t, pl.ds(2 * k, 2)].reshape(128, 512).astype(F32))

            square = squares[...]
            upper = square.astype(BF16)
            lower = (square - upper.astype(F32)).astype(BF16)
            n1[0] = jnp.where(row == k, dot_t(ones, upper) + dot_t(ones, lower), n1[0])

    norm1 = remote(n1.at[0], n1.at[1], send1.at[1], recv1.at[1], to_core)
    norm1.start()
    stage1.wait_recv()

    @pl.loop(0, 2)
    def _(k):
        s2[k] = (mine[k, :, 1 - half, core] + r1[k, :, 1 - half].astype(F32)).astype(BF16)

    stage2 = remote(s2, r2, send2.at[0], recv2.at[0], to_half)
    stage2.start()
    norm1.wait_recv()
    n2[0] = n1[0] + n1[1]
    norm2 = remote(n2.at[0], n2.at[1], send2.at[1], recv2.at[1], to_half)
    norm2.start()

    norm2.wait_recv()
    inverse = lax.rsqrt(n2[0] + n2[1] + EPS)
    lane = lax.broadcasted_iota(jnp.int32, (32, 128), 1)
    at = lax.broadcasted_iota(jnp.int32, (32, 128), 0) + (half * 2 + core) * 32
    factor = F32(FEATURES) ** 0.5
    columns = []
    for r in range(ROUNDS):
        spread = jnp.broadcast_to(inverse[4 + r:5 + r], (32, 128))
        columns.append(jnp.sum(jnp.where(lane == at, spread, 0.0), axis=1, keepdims=True))
    stage2.wait_recv()
    for k in range(4):
        lanes = slice(128 * (k % 2), 128 * (k % 2) + 128)
        tiles = []
        for r in range(ROUNDS):
            gram = mine[k // 2, r, half, core, :, lanes] + r1[k // 2, r, half, :, lanes].astype(F32)
            gram = gram + r2[k // 2, r, :, lanes].astype(F32)
            tiles.append(gram * inverse[k:k + 1] * columns[r] * factor)
        lanes = slice(128 * k, 128 * k + 128)
        out_ref[0, :, lanes] = lax.select(swap, tiles[1], tiles[0])
        out_ref[1, :, lanes] = lax.select(swap, tiles[0], tiles[1])

    for copy in (stage1, norm1, stage2, norm2):
        copy.wait_send()

    @pl.loop(0, NY)
    def _(t):
        @pl.when(t > 0)
        def _():
            wide_copy(t).wait_send()
            for h in range(2):
                piece_copy(t, h).wait_send()

        @pl.loop(1, NX)
        def _(s):
            x_copy(t, s).wait_send()

        for r in moved:
            z_copy(t, r).wait_send()


def tiles(number, shifts, pairing, values, scales):
    dma = pltpu.SemaphoreType.DMA
    rows = (2, 2, 32, 512)
    return pl.pallas_call(
        functools.partial(kernel, shifts),
        out_shape=jax.ShapeDtypeStruct((ROUNDS, 32, 512), F32),
        in_specs=[SMEM, VMEM, VMEM],
        out_specs=VMEM,
        scratch_shapes=[
            pltpu.VMEM((NY, 2 * NY + 2 * ROUNDS, 2, 32, 512), BF16),
            pltpu.VMEM((NY,) + rows, BF16),
            pltpu.VMEM((NY, NX - 1) + rows, BF16),
            pltpu.VMEM((NY, ROUNDS) + rows, BF16),
            pltpu.VMEM((2, ROUNDS, 2, 2, 32, 256), F32),
            pltpu.VMEM((128, 512), F32),
            pltpu.VMEM((2, ROUNDS, 2, 32, 256), BF16),
            pltpu.VMEM((2, ROUNDS, 2, 32, 256), BF16),
            pltpu.VMEM((2, ROUNDS, 32, 256), BF16),
            pltpu.VMEM((2, ROUNDS, 32, 256), BF16),
            pltpu.VMEM((2, 8, 128), F32),
            pltpu.VMEM((2, 8, 128), F32),
            dma((NY - 1, 2)), dma((NY - 1, 2)),
            dma((NY, NX - 1)), dma((NY, NX - 1)),
            dma((NY - 1,)), dma((NY - 1,)),
            dma((NY, ROUNDS)), dma((NY, ROUNDS)),
            dma((2,)), dma((2,)), dma((2,)), dma((2,)),
        ],
        compiler_params=pltpu.CompilerParams(
            collective_id=number, has_side_effects=True, vmem_limit_bytes=32 * 1024 * 1024),
        name=f"tiles_{shifts[0]}_{shifts[1]}",
    )(pairing, values, scales)


def local(values, scales, pairing):
    cases = [(low, high) for high in range(NZ) for low in range(high + 1)]
    digits = jnp.bitwise_and(pairing, NZ - 1)
    swapped = digits[::-1]
    low, high = jnp.minimum(digits, swapped), jnp.maximum(digits, swapped)
    case = (jnp.right_shift(high * (high + 1), 1) + low)[0]
    branches = [functools.partial(tiles, number, shifts) for number, shifts in enumerate(cases)]
    return jnp.swapaxes(lax.switch(case, branches, pairing, values, scales), 1, 2)


def solution(mesh):
    placed = (P("blk", "feat"), P("blk", "feat"), P())
    return jax.shard_map(
        local, mesh=mesh, in_specs=placed, out_specs=P(None, "blk", "feat"), check_vma=False
    )
```

```python
import functools

import jax
import jax.numpy as jnp
from jax import lax
from jax.experimental import pallas as pl
from jax.experimental.pallas import tpu as pltpu
from jax.sharding import PartitionSpec as P

FEATURES = 8192
GROUP = 128
ROUNDS = 2
EPS = 1e-06
NX, NZ = 4, 8
NY = 4
MESH = pl.DeviceIdType.MESH
VMEM = pl.BlockSpec(memory_space=pltpu.VMEM)
SMEM = pl.BlockSpec(memory_space=pltpu.SMEM)
BF16, F32 = jnp.bfloat16, jnp.float32


def dot_t(a, b):
    return lax.dot_general(a, b, (((1,), (1,)), ((), ())), preferred_element_type=F32)


def rank(digit, least, pick):
    return 2 * least(digit, NZ - digit) + pick(digit > NZ // 2, 1, 0)


def kernel(shifts, pairing_ref, values_ref, scales_ref, out_ref,
           held, piece, near, stage, mine, squares, done, s1, r1, s2, r2, n1, n2,
           send_p, recv_p, send_x, recv_x, send_w, recv_w, send_z, recv_z, send1, recv1, send2, recv2):
    blk, feat = lax.axis_index("blk"), lax.axis_index("feat")
    x, z = blk // NZ, lax.rem(blk, NZ)
    half, y, core = feat // 8, lax.rem(feat // 2, NY), lax.rem(feat, 2)
    to_core = (blk, feat + 1 - 2 * core)
    to_half = (blk, feat + 8 - 16 * half)
    own = held.at[0, pl.ds(0, 2 * NY)]
    moved = [r for r in range(ROUNDS) if shifts[r]]

    def at_y(t):
        return lax.rem(y + NY - t, NY)

    def to_y(t):
        return (blk, feat + 2 * (at_y(t) - y))

    def to_x(s):
        return (lax.rem(x + NX - s, NX) * NZ + z, feat)

    def to_z(d):
        return (x * NZ + lax.rem(z + NZ - d, NZ), feat)

    barrier = pltpu.get_barrier_semaphore()
    sources = [to_z(NZ - d) for d in sorted(set(shifts)) if d]
    peers = [to_y(t) for t in range(1, NY)] + [to_x(s) for s in range(1, NX)] + sources + [to_core, to_half]
    for peer in peers:
        pl.semaphore_signal(barrier, inc=1, device_id=peer, device_id_type=MESH)

    def remote(src, dst, send, recv, peer):
        return pltpu.make_async_remote_copy(
            src_ref=src, dst_ref=dst, send_sem=send, recv_sem=recv, device_id=peer, device_id_type=MESH)

    def piece_copy(t, h):
        return remote(held.at[0, h * NY + at_y(t)], piece.at[t, h],
                      send_p.at[t - 1, h], recv_p.at[t - 1, h], to_y(t))

    def wide_copy(t):
        return remote(own, held.at[t, pl.ds(0, 2 * NY)], send_w.at[t - 1], recv_w.at[t - 1], to_y(t))

    def x_copy(t, h, s):
        return remote(piece.at[t, h], near.at[t, s - 1, h], send_x.at[t, h, s - 1], recv_x.at[t, h, s - 1], to_x(s))

    def z_copy(t, h, r):
        shift = shifts[r] if isinstance(r, int) else jnp.where(r == 0, shifts[0], shifts[1])
        return remote(stage.at[t, r, h], held.at[t, 2 * NY + 2 * r + h], send_z.at[t, h, r], recv_z.at[t, h, r],
                      to_z(shift))

    @pl.loop(0, 2 * NY)
    def _(q):
        rows = pl.ds(q * 64, 64)
        for g in range(values_ref.shape[1] // GROUP):
            lanes = slice(g * GROUP, (g + 1) * GROUP)
            part = (values_ref[rows, lanes].astype(F32) * scales_ref[rows, g:g + 1]).astype(BF16)
            held[0, q, :, :, lanes] = part.reshape(2, 32, GROUP)

    for h in range(2):
        piece[0, h] = held[0, h * NY + y]
    pl.semaphore_wait(barrier, len(peers))

    first = pairing_ref[0]
    second = pairing_ref[1]
    swap = rank(lax.rem(first, NZ), jnp.minimum, jnp.where) > rank(lax.rem(second, NZ), jnp.minimum, jnp.where)
    offsets = [jnp.where(swap, second, first), jnp.where(swap, first, second)]
    picks = [lax.rem(offsets[r] // NZ + jnp.where(z < shifts[r], 1, 0), NX) for r in range(ROUNDS)]

    @pl.loop(0, 2 * NY + 1)
    def _(step):
        later, side = step // 2, lax.rem(step, 2)

        @pl.when(jnp.logical_and(step > 1, step < 2 * NY))
        def _():
            piece_copy(later, side).wait_recv()

        @pl.when(step < 2 * NY)
        def _():
            @pl.loop(1, NX)
            def _(s):
                x_copy(later, side, s).start()

        @pl.when(step == 0)
        def _():
            @pl.loop(1, NY)
            def _(t):
                for h in range(2):
                    piece_copy(t, h).start()

        @pl.when(step == 1)
        def _():
            @pl.loop(1, NY)
            def _(t):
                wide_copy(t).start()

        @pl.when(step > 0)
        def _():
            t, h = (step - 1) // 2, lax.rem(step - 1, 2)

            @pl.loop(1, NX)
            def _(s):
                x_copy(t, h, s).wait_recv()

            for r in range(ROUNDS):
                @pl.loop(0, 2)
                def _(c):
                    value = piece[t, h, c]
                    for s in range(1, NX):
                        value = lax.select(picks[r] == s, near[t, s - 1, h, c], value)
                    if shifts[r]:
                        stage[t, r, h, c] = value
                    else:
                        held[t, 2 * NY + 2 * r + h, c] = value

                if shifts[r]:
                    z_copy(t, h, r).start()

    @pl.loop(1, NY)
    def _(t):
        wide_copy(t).wait_recv()

    @pl.loop(0, ROUNDS)
    def _(r):
        n1[r, 0] = jnp.zeros((8, 128), F32)
        for k in range(2):
            mine[r, k] = jnp.zeros(mine.shape[2:], F32)

    ones = jnp.ones((8, 512), BF16)
    row = lax.broadcasted_iota(jnp.int32, (8, 128), 0)

    def stage1(r):
        return remote(s1.at[r], r1.at[r], send1.at[r, 0], recv1.at[r, 0], to_core)

    def norm1(r):
        return remote(n1.at[r, 0], n1.at[r, 1], send1.at[r, 1], recv1.at[r, 1], to_core)

    def stage2(r):
        return remote(s2.at[r], r2.at[r], send2.at[r, 0], recv2.at[r, 0], to_half)

    def norm2(r):
        return remote(n2.at[r, 0], n2.at[r, 1], send2.at[r, 1], recv2.at[r, 1], to_half)

    @pl.loop(0, ROUNDS + 1)
    def _(turn):
        r = jnp.maximum(turn - 1, 0)

        @pl.when(turn > 0)
        def _():
            @pl.loop(0, NY)
            def _(t):
                for h in range(2):
                    if len(moved) == ROUNDS:
                        z_copy(t, h, r).wait_recv()
                    elif moved:
                        @pl.when(r == moved[0])
                        def _(h=h):
                            z_copy(t, h, moved[0]).wait_recv()
                rows = held[t, pl.ds(2 * NY + 2 * r, 2)].reshape(128, 512)

                @pl.loop(0, 2)
                def _(k):
                    owns = held[t, pl.ds(k * NY, NY)].reshape(256, 512)
                    mine[r, k] += dot_t(rows, owns).reshape(2, 2, 32, 256)

            for k in range(2):
                s1[r, k] = mine[r, k, :, 1 - core].astype(BF16)
            stage1(r).start()

        @pl.loop(jnp.where(turn == 0, 0, 3 + turn), 4 + turn)
        def _(k):
            squares[...] = jnp.zeros_like(squares)

            @pl.loop(0, NY)
            def _(t):
                squares[...] += jnp.square(held[t, pl.ds(2 * k, 2)].reshape(128, 512).astype(F32))

            square = squares[...]
            upper = square.astype(BF16)
            lower = (square - upper.astype(F32)).astype(BF16)
            n1[r, 0] = jnp.where(row == k, dot_t(ones, upper) + dot_t(ones, lower), n1[r, 0])

        @pl.when(turn > 0)
        def _():
            norm1(r).start()
            stage1(r).wait_recv()
            for k in range(2):
                s2[r, k] = (mine[r, k, 1 - half, core] + r1[r, k, 1 - half].astype(F32)).astype(BF16)
            stage2(r).start()
            norm1(r).wait_recv()
            n2[r, 0] = n1[r, 0] + n1[r, 1]
            norm2(r).start()

    lane = lax.broadcasted_iota(jnp.int32, (32, 128), 1)
    at = lax.broadcasted_iota(jnp.int32, (32, 128), 0) + (half * 2 + core) * 32
    factor = F32(FEATURES) ** 0.5

    @pl.loop(0, ROUNDS)
    def _(r):
        norm2(r).wait_recv()
        across = lax.rsqrt(n2[0, 0] + n2[0, 1] + EPS)
        down = lax.rsqrt(n2[r, 0] + n2[r, 1] + EPS)
        down = jnp.sum(jnp.where(row == 4 + r, down, 0.0), axis=0, keepdims=True)
        spread = jnp.broadcast_to(down, (32, 128))
        column = jnp.sum(jnp.where(lane == at, spread, 0.0), axis=1, keepdims=True)
        stage2(r).wait_recv()
        for k in range(4):
            lanes = slice(128 * (k % 2), 128 * (k % 2) + 128)
            gram = mine[r, k // 2, half, core, :, lanes] + r1[r, k // 2, half, :, lanes].astype(F32)
            gram = gram + r2[r, k // 2, :, lanes].astype(F32)
            done[r, k] = gram * across[k:k + 1] * column * factor

    for k in range(4):
        lanes = slice(128 * k, 128 * k + 128)
        out_ref[0, :, lanes] = lax.select(swap, done[1, k], done[0, k])
        out_ref[1, :, lanes] = lax.select(swap, done[0, k], done[1, k])

    @pl.loop(0, ROUNDS)
    def _(r):
        for copy in (stage1(r), norm1(r), stage2(r), norm2(r)):
            copy.wait_send()

    @pl.loop(0, NY)
    def _(t):
        @pl.when(t > 0)
        def _():
            wide_copy(t).wait_send()
            for h in range(2):
                piece_copy(t, h).wait_send()

        for h in range(2):
            @pl.loop(1, NX)
            def _(s, h=h):
                x_copy(t, h, s).wait_send()

            for r in moved:
                z_copy(t, h, r).wait_send()


def tiles(number, shifts, pairing, values, scales):
    dma = pltpu.SemaphoreType.DMA
    rows = (2, 2, 32, 512)
    return pl.pallas_call(
        functools.partial(kernel, shifts),
        out_shape=jax.ShapeDtypeStruct((ROUNDS, 32, 512), F32),
        in_specs=[SMEM, VMEM, VMEM],
        out_specs=VMEM,
        scratch_shapes=[
            pltpu.VMEM((NY, 2 * NY + 2 * ROUNDS, 2, 32, 512), BF16),
            pltpu.VMEM((NY,) + rows, BF16),
            pltpu.VMEM((NY, NX - 1) + rows, BF16),
            pltpu.VMEM((NY, ROUNDS) + rows, BF16),
            pltpu.VMEM((ROUNDS, 2, 2, 2, 32, 256), F32),
            pltpu.VMEM((128, 512), F32),
            pltpu.VMEM((ROUNDS, 4, 32, 128), F32),
            pltpu.VMEM((ROUNDS, 2, 2, 32, 256), BF16),
            pltpu.VMEM((ROUNDS, 2, 2, 32, 256), BF16),
            pltpu.VMEM((ROUNDS, 2, 32, 256), BF16),
            pltpu.VMEM((ROUNDS, 2, 32, 256), BF16),
            pltpu.VMEM((ROUNDS, 2, 8, 128), F32),
            pltpu.VMEM((ROUNDS, 2, 8, 128), F32),
            dma((NY - 1, 2)), dma((NY - 1, 2)),
            dma((NY, 2, NX - 1)), dma((NY, 2, NX - 1)),
            dma((NY - 1,)), dma((NY - 1,)),
            dma((NY, 2, ROUNDS)), dma((NY, 2, ROUNDS)),
            dma((ROUNDS, 2)), dma((ROUNDS, 2)), dma((ROUNDS, 2)), dma((ROUNDS, 2)),
        ],
        compiler_params=pltpu.CompilerParams(
            collective_id=number, has_side_effects=True, vmem_limit_bytes=32 * 1024 * 1024),
        name=f"tiles_{shifts[0]}_{shifts[1]}",
    )(pairing, values, scales)


def local(values, scales, pairing):
    order = functools.partial(rank, least=min, pick=lambda flag, yes, no: yes if flag else no)
    cases = [tuple(sorted((low, high), key=order)) for high in range(NZ) for low in range(high + 1)]
    digits = jnp.bitwise_and(pairing, NZ - 1)
    swapped = digits[::-1]
    low, high = jnp.minimum(digits, swapped), jnp.maximum(digits, swapped)
    case = (jnp.right_shift(high * (high + 1), 1) + low)[0]
    branches = [functools.partial(tiles, number, shifts) for number, shifts in enumerate(cases)]
    return jnp.swapaxes(lax.switch(case, branches, pairing, values, scales), 1, 2)


def solution(mesh):
    placed = (P("blk", "feat"), P("blk", "feat"), P())
    return jax.shard_map(
        local, mesh=mesh, in_specs=placed, out_specs=P(None, "blk", "feat"), check_vma=False
    )
```
